32 devices in a mesh: section: 16 (over z, y, core), tensor: 2 (over x).
Axes of the slice: x: 2, y: 2, z: 4, core: 2. Of those that a mesh axis runs over, the one named last changes fastest.
Arguments:
- queries: bfloat16 [2048, 3072], P('section', 'tensor'), may hold values from -6 to 6
- keys: bfloat16 [2048, 3072], P('section', 'tensor'), may hold values from -6 to 6
- values: bfloat16 [2048, 3072], P('section', 'tensor'), may hold values from -6 to 6
- latents: float32 [1024, 128], P('section'), may hold values from -6 to 6
- out_weight: bfloat16 [3072, 3072], P('tensor'), may hold values from -1 to 1
- gain: float32 [3072], P('tensor'), may hold values from 0.1 to 1.9
- head_weight: bfloat16 [3072, 64], P('tensor'), may hold values from -0.109375 to 0.109375
- levels: int32 [8], replicated, may hold values from 0 to 7, each once
- timesteps: int32 [9], replicated, may hold values from 0 to 1000, as said below
- order: int32 [8], replicated, may hold values from 0 to 7, each once
Outputs:
- velocity: float32 [1024, 128], P('section')
- advanced: float32 [1024, 128], P('section')
The draws below stay inside these ranges and needn't reach their ends.
Inputs may be any that keep to these rules, and one draw needn't show every extreme that they name: timesteps fall strictly from 1000 at index 0 to 0 at index 8.
All inputs are finite; a program needn't handle non-finite values.
Results may differ from the reference program's by a relative error of at most 0.004.
Values may be sent and summed in bfloat16 or wider, within the bound.
No kernel may reach another device: no remote copies, remote signals or barrier semaphores. Data moves between devices by JAX's collectives and lax.ppermute only.
A program may use at most 128 MiB of HBM per device.

```python
import math
import jax
import jax.numpy as jnp
from jax import lax

D = 3072
HEADS = 24
HD = 128
LAT = 64
GROUPS = 8
TOKENS = 2048
LEVELS = 8


def draw_queries(key, part):
    key = jax.random.fold_in(key, 3)
    return jnp.clip(1.5 * jax.random.normal(key, (TOKENS, HEADS * HD), jnp.float32), -6.0, 6.0).astype(jnp.bfloat16)


def draw_keys(key, part):
    key = jax.random.fold_in(key, 5)
    return jnp.clip(1.5 * jax.random.normal(key, (TOKENS, HEADS * HD), jnp.float32), -6.0, 6.0).astype(jnp.bfloat16)


def draw_values(key, part):
    key = jax.random.fold_in(key, 11)
    group_of = jnp.arange(TOKENS, dtype=jnp.int32) // (TOKENS // GROUPS)
    group_scale = jnp.exp(jax.random.uniform(jax.random.fold_in(key, 12), (GROUPS,), jnp.float32, math.log(0.15), math.log(2.0)))
    token_scale = jax.random.uniform(jax.random.fold_in(key, 13), (TOKENS,), jnp.float32, 0.5, 1.5)
    strength = group_scale[group_of] * token_scale
    base = jax.random.normal(key, (TOKENS, HEADS * HD), jnp.float32)
    shared = jax.random.normal(jax.random.fold_in(key, 14), (GROUPS, HD), jnp.float32)
    shared_rows = jnp.tile(shared[group_of], (1, HEADS))
    return jnp.clip(base + strength[:, None] * shared_rows, -6.0, 6.0).astype(jnp.bfloat16)


def draw_out_weight(key, part):
    key = jax.random.fold_in(key, 7)
    column = jnp.arange(D, dtype=jnp.float32) / D
    head_gain = jax.random.uniform(jax.random.fold_in(key, 8), (HEADS,), jnp.float32, 0.5, 1.5)
    base = jnp.clip(jax.random.normal(key, (HEADS * HD, D), jnp.float32), -6.0, 6.0)
    rise = jnp.exp(column * math.log(10.0))
    common = jnp.clip(jax.random.normal(jax.random.fold_in(key, 10), (HD, D), jnp.float32), -6.0, 6.0)
    amplitude = 5.0
    shared = (head_gain[:, None, None] * common[None, :, :]).reshape(HEADS * HD, D)
    total = base * rise[None, :] + amplitude * shared / math.sqrt(HEADS)
    return (total / math.sqrt(HEADS * HD * 400.0)).astype(jnp.bfloat16)


def draw_timesteps(key, part):
    key = jax.random.fold_in(key, 9)
    increments = jax.random.randint(key, (LEVELS,), 1, 10)
    running = jnp.concatenate([jnp.zeros((1,), jnp.int32), jnp.cumsum(increments).astype(jnp.int32)])
    return 1000 - running * 1000 // running[-1]


def block_levels(key, dims, shards, least, high):
    factor_of = 1.0
    for position, parts in shards:
        draws = jax.random.uniform(jax.random.fold_in(jax.random.fold_in(key, 6), position), (parts,), jnp.float32, least / len(shards), high / len(shards))
        factor_of = factor_of * jnp.repeat(jnp.exp(draws), dims[position] // parts).reshape((-1,) + (1,) * (len(dims) - 1 - position))
    return factor_of


def centred(rng, dims, scale, limit, shards=(), held_as=jnp.bfloat16):
    values = scale * jax.random.normal(rng, dims, jnp.float32)
    if shards:
        values = values * block_levels(rng, dims, shards, -0.22, 0.18)
    return jnp.clip(values, -limit, limit).astype(held_as)


def setup_inputs(seed: int = 0) -> dict:
    streams_of = jax.random.split(jax.random.key(seed), 11)
    queries = draw_queries(jax.random.fold_in(streams_of[10], 71), 0)
    keys = draw_keys(jax.random.fold_in(streams_of[10], 71), 0)
    values = draw_values(jax.random.fold_in(streams_of[10], 71), 0)
    latents = centred(streams_of[3], (TOKENS // 2, 2 * LAT), 1.0, 6.0, ((0, 16),), jnp.float32)
    out_weight = draw_out_weight(jax.random.fold_in(streams_of[10], 71), 0)
    gain = jnp.clip(1.0 + 0.18 * jax.random.normal(streams_of[5], (D,), jnp.float32), 0.1, 1.9)
    head_weight = centred(streams_of[6], (D, LAT), D ** -0.5, 0.109375, ((0, 2),))
    levels = jax.random.permutation(streams_of[7], GROUPS).astype(jnp.int32)
    timesteps = draw_timesteps(jax.random.fold_in(streams_of[10], 71), 0)
    order = jax.random.permutation(streams_of[9], GROUPS).astype(jnp.int32)
    return dict(queries=queries, keys=keys, values=values, latents=latents, out_weight=out_weight, gain=gain, head_weight=head_weight, levels=levels, timesteps=timesteps, order=order)


def reference(queries, keys, values, latents, out_weight, gain, head_weight, levels, timesteps, order):
    tok_count = queries.shape[0]
    group_rows = tok_count // GROUPS
    group_of = jnp.arange(tok_count, dtype=jnp.int32) // group_rows
    tok_order = order[group_of]
    visible = tok_order[None, :] <= tok_order[:, None]
    factor = 1.0 / math.sqrt(HD)

    def split_heads(matrix):
        return matrix.astype(jnp.float32).reshape(tok_count, HEADS, HD).transpose(1, 0, 2)

    def one_head(operands):
        query_head, key_head, value_head = operands
        scores = jnp.dot(query_head, key_head.T, precision=lax.Precision.HIGHEST) * factor
        masked = jnp.where(visible, scores, -1e+30)
        top = lax.optimization_barrier(jnp.max(masked, axis=1, keepdims=True))
        weights = jnp.where(visible, jnp.exp(masked - top), 0.0)
        prob_total = lax.optimization_barrier(jnp.sum(weights, axis=1, keepdims=True))
        rounded = lax.optimization_barrier(weights.astype(jnp.bfloat16)).astype(jnp.float32)
        return jnp.dot(rounded, value_head, precision=lax.Precision.HIGHEST) / prob_total
    attended = lax.map(one_head, (split_heads(queries), split_heads(keys), split_heads(values)))
    attended = attended.transpose(1, 0, 2).reshape(tok_count, HEADS * HD).astype(jnp.bfloat16)
    projected = jnp.dot(attended, out_weight, preferred_element_type=jnp.float32)
    mean_square = lax.optimization_barrier(jnp.mean(projected * projected, axis=1, keepdims=True))
    scaled = (projected * gain[None, :]).astype(jnp.bfloat16)
    head_raw = jnp.dot(scaled, head_weight, preferred_element_type=jnp.float32)
    velocity = head_raw * lax.rsqrt(mean_square + 1e-06)
    group_level = levels[group_of]
    delta = (timesteps[group_level + 1] - timesteps[group_level]).astype(jnp.float32) / 1000.0
    moved = latents.reshape(tok_count, LAT) + delta[:, None] * velocity
    advanced = jnp.roll(moved, group_rows, axis=0)
    return (velocity.reshape(tok_count // 2, 2 * LAT), advanced.reshape(tok_count // 2, 2 * LAT))
```

```python
import functools
import math

import jax
import jax.numpy as jnp
from jax import lax
from jax.experimental import pallas as pl
from jax.experimental.pallas import tpu as pltpu
from jax.sharding import PartitionSpec as P

HD = 128
GROUPS = 8
MAX_HEAD_SPLIT = 4
NEG = -1e30
VMEM = pl.BlockSpec(memory_space=pltpu.VMEM)
SMEM = pl.BlockSpec(memory_space=pltpu.SMEM)


def params(mib):
    return pltpu.CompilerParams(vmem_limit_bytes=mib * 1024 * 1024)


def struct(shape, dtype):
    return jax.ShapeDtypeStruct(shape, dtype)


class Plan:
    def __init__(self, queries):
        self.sections = lax.axis_size("section")
        self.tensors = lax.axis_size("tensor")
        self.rows, self.width = queries.shape
        self.heads = self.width // HD
        self.split = math.gcd(self.heads, MAX_HEAD_SPLIT)
        self.members = self.sections // self.split
        self.cols = self.width // self.split
        self.span = self.sections // GROUPS
        self.share = self.rows // self.tensors

    def part(self):
        return lax.axis_index("section") // self.members

    def to_part(self, value, step):
        pairs = [(s, s ^ (step * self.members)) for s in range(self.sections)]
        return lax.ppermute(value, "section", pairs)

    def to_member(self, value, step):
        return lax.ppermute(value, "section", [(s, s ^ step) for s in range(self.sections)])

    def to_tensor(self, value, step):
        return lax.ppermute(value, "tensor", [(t, t ^ step) for t in range(self.tensors)])

    def to_next_group(self, value, step):
        pairs = [
            (s * self.tensors + t, ((s + self.span) % self.sections) * self.tensors + (t ^ step))
            for s in range(self.sections)
            for t in range(self.tensors)
        ]
        return lax.ppermute(value, ("section", "tensor"), pairs)

    def gather_members(self, piece):
        pieces = {0: piece}
        step = self.members // 2
        while step:
            pieces.update({i ^ step: self.to_member(v, step) for i, v in list(pieces.items())})
            step //= 2
        return [pieces[i] for i in range(self.members)]


def pack_kernel(plan, arrays, *refs):
    sources, targets = refs[:arrays], refs[arrays:]
    part = plan.part()
    for step, target in enumerate(targets):
        here = pl.ds(pl.multiple_of((part ^ step) * plan.cols, 128), plan.cols)
        for i, source in enumerate(sources):
            target[pl.ds(i * plan.rows, plan.rows), :] = source[:, here]


def pack(plan, *arrays):
    return pl.pallas_call(
        functools.partial(pack_kernel, plan, len(arrays)),
        out_shape=[struct((len(arrays) * plan.rows, plan.cols), jnp.bfloat16)] * plan.split,
        in_specs=[VMEM] * len(arrays),
        out_specs=[VMEM] * plan.split,
        compiler_params=params(32),
    )(*arrays)


def attend_kernel(plan, steps, order_ref, *refs):
    rows = plan.rows
    queries, refs = refs[: len(steps)], refs[len(steps) :]
    count = plan.split * plan.members
    pieces, refs = refs[:count], refs[count:]
    outs, scores = refs[: len(steps)], refs[len(steps)]
    me = lax.axis_index("section")
    factor = 1.0 / math.sqrt(HD)
    many = len(steps) * rows
    width = 2 * rows if plan.span % 2 == 0 and plan.members % 2 == 0 else rows
    per = width // rows
    blocks = [pieces[i : i + per] for i in range(0, count, per)]

    def order_of(step, member):
        return order_ref[(me ^ (step * plan.members + member)) // plan.span]

    own = [order_of(step, 0) for step in steps]
    for h in range(plan.cols // HD):
        lanes = pl.ds(h * HD, HD)
        q = jnp.concatenate([ref[:, lanes] for ref in queries], axis=0)
        top = None
        for j, block in enumerate(blocks):
            k = jnp.concatenate([ref[pl.ds(0, rows), lanes] for ref in block], axis=0)
            s = lax.dot_general(q, k, (((1,), (1,)), ((), ())), preferred_element_type=jnp.float32)
            first = j * per
            key_order = order_of(first // plan.members, first % plan.members)
            s = jnp.concatenate(
                [
                    s[i * rows : (i + 1) * rows] * factor + jnp.where(key_order <= o, 0.0, NEG)
                    for i, o in enumerate(own)
                ],
                axis=0,
            )
            scores[:, pl.ds(j * width, width)] = s
            top = s if top is None else jnp.maximum(top, s)
        top = jnp.max(top, axis=1, keepdims=True)
        total = jnp.zeros((many, width), jnp.float32)
        summed = jnp.zeros((many, HD), jnp.float32)
        for j, block in enumerate(blocks):
            v = jnp.concatenate([ref[pl.ds(rows, rows), lanes] for ref in block], axis=0)
            w = jnp.exp(scores[:, pl.ds(j * width, width)] - top)
            total += w
            summed += jnp.dot(w.astype(jnp.bfloat16), v, preferred_element_type=jnp.float32)
        out = (summed / jnp.sum(total, axis=1, keepdims=True)).astype(jnp.bfloat16)
        for i, ref in enumerate(outs):
            ref[:, lanes] = out[i * rows : (i + 1) * rows]


def attend(plan, steps, order, queries, pieces):
    return pl.pallas_call(
        functools.partial(attend_kernel, plan, steps),
        out_shape=[struct((plan.rows, plan.cols), jnp.bfloat16)] * len(steps),
        in_specs=[SMEM] + [VMEM] * (len(steps) + len(pieces)),
        out_specs=[VMEM] * len(steps),
        scratch_shapes=[pltpu.VMEM((len(steps) * plan.rows, len(pieces) * plan.rows), jnp.float32)],
        compiler_params=params(48),
        cost_estimate=pl.CostEstimate(
            flops=4 * len(steps) * plan.rows * len(pieces) * plan.rows * plan.cols,
            bytes_accessed=4 * len(pieces) * plan.rows * plan.cols,
            transcendentals=len(steps) * plan.rows * len(pieces) * plan.rows * plan.cols // HD,
        ),
    )(order, *queries, *pieces)


def project_kernel(plan, *refs):
    parts, weight = refs[: plan.split], refs[plan.split]
    outs = refs[plan.split + 1 :]
    part, tensor = plan.part(), lax.axis_index("tensor")
    total = None
    for step, ref in enumerate(parts):
        here = pl.ds(pl.multiple_of((part ^ step) * plan.cols, 128), plan.cols)
        term = jnp.dot(ref[...], weight[here, :], preferred_element_type=jnp.float32)
        total = term if total is None else total + term
    full = refs[-1]
    full[...] = total
    for step, out in enumerate(outs[:-1]):
        here = pl.ds(pl.multiple_of((tensor ^ step) * plan.share, 8), plan.share)
        out[...] = full[here, :].astype(out.dtype)


def project(plan, parts, weight):
    width = weight.shape[1]
    tile = 512
    shapes = [struct((plan.share, width), jnp.float32)]
    shapes += [struct((plan.share, width), jnp.bfloat16)] * (plan.tensors - 1)
    return pl.pallas_call(
        functools.partial(project_kernel, plan),
        grid=(width // tile,),
        out_shape=shapes,
        in_specs=[pl.BlockSpec((plan.rows, plan.cols), lambda i: (0, 0))] * plan.split
        + [pl.BlockSpec((weight.shape[0], tile), lambda i: (0, i))],
        out_specs=[pl.BlockSpec((plan.share, tile), lambda i: (0, i))] * plan.tensors,
        scratch_shapes=[pltpu.VMEM((plan.rows, tile), jnp.float32)],
        compiler_params=params(32),
    )(*parts, weight)


def head_kernel(plan, levels, timesteps, *refs):
    sums, refs = refs[: plan.tensors], refs[plan.tensors :]
    gains, refs = refs[: plan.tensors], refs[plan.tensors :]
    heads, refs = refs[: plan.tensors], refs[plan.tensors :]
    latents, velocity_ref, moved_ref, full, rows = refs
    tensor = lax.axis_index("tensor")
    total = sums[0][...]
    for ref in sums[1:]:
        total = total + ref[...].astype(jnp.float32)
    full[...] = total
    squares = jnp.sum(total * total, axis=1, keepdims=True)
    raw = None
    for step in range(plan.tensors):
        share = gains[step].shape[1]
        here = pl.ds(pl.multiple_of((tensor ^ step) * share, 128), share)
        scaled = (full[:, here] * gains[step][...]).astype(jnp.bfloat16)
        term = jnp.dot(scaled, heads[step][...], preferred_element_type=jnp.float32)
        raw = term if raw is None else raw + term
    rows[...] = raw * lax.rsqrt(squares / total.shape[1] + 1e-6)
    half = plan.share // 2
    velocity = jnp.concatenate(
        [rows[pl.ds(0, half, 2), :], rows[pl.ds(1, half, 2), :]], axis=1
    )
    level = levels[lax.axis_index("section") // plan.span]
    change = (timesteps[level + 1] - timesteps[level]).astype(jnp.float32)
    delta = jnp.full(velocity.shape, change, jnp.float32) / 1000.0
    velocity_ref[...] = velocity
    here = pl.ds(pl.multiple_of(tensor * half, 8), half)
    moved_ref[...] = latents[here, :] + delta * velocity


def head(plan, levels, timesteps, sums, gains, heads, latents):
    half = struct((plan.share // 2, latents.shape[1]), jnp.float32)
    return pl.pallas_call(
        functools.partial(head_kernel, plan),
        out_shape=[half, half],
        in_specs=[SMEM, SMEM] + [VMEM] * (3 * plan.tensors + 1),
        out_specs=[VMEM, VMEM],
        scratch_shapes=[
            pltpu.VMEM(sums[0].shape, jnp.float32),
            pltpu.VMEM((plan.share, heads[0].shape[1]), jnp.float32),
        ],
        compiler_params=params(32),
    )(levels, timesteps, *sums, *gains, *heads, latents)


def place_kernel(plan, *refs):
    velocities, moved = refs[: plan.tensors], refs[plan.tensors : 2 * plan.tensors]
    tensor = lax.axis_index("tensor")
    for parts, out in ((velocities, refs[-2]), (moved, refs[-1])):
        for step, ref in enumerate(parts):
            rows = ref.shape[0]
            out[pl.ds(pl.multiple_of((tensor ^ step) * rows, 8), rows), :] = ref[...]


def place(plan, velocities, moved):
    shape = struct((plan.rows // 2, velocities[0].shape[1]), jnp.float32)
    return pl.pallas_call(
        functools.partial(place_kernel, plan),
        out_shape=[shape, shape],
        in_specs=[VMEM] * (2 * plan.tensors),
        out_specs=[VMEM, VMEM],
    )(*velocities, *moved)


def local(queries, keys, values, latents, out_weight, gain, head_weight, levels, timesteps, order):
    plan = Plan(queries)
    split, tensors = plan.split, plan.tensors

    sent = pack(plan, keys, values)
    key_values = [sent[0]] + [plan.to_part(sent[i], i) for i in range(1, split)]
    sent = pack(plan, queries)
    asked = [sent[0]] + [plan.to_part(sent[i], i) for i in range(1, split)]
    gains = [gain[None, :]]
    heads = [head_weight]
    gains += [plan.to_tensor(gains[0], i) for i in range(1, tensors)]
    heads += [plan.to_tensor(heads[0], i) for i in range(1, tensors)]
    pieces = [p for piece in key_values for p in plan.gather_members(piece)]

    far = list(range(split // 2, split))
    near = list(range(split // 2))
    attended = [None] * split
    for steps in (far, near):
        if steps:
            outs = attend(plan, steps, order, [asked[i] for i in steps], pieces)
            for i, out in zip(steps, outs):
                attended[i] = plan.to_part(out, i) if i else out

    sums = project(plan, attended, out_weight)
    sums = [sums[0]] + [plan.to_tensor(sums[i], i) for i in range(1, tensors)]
    velocity, moved = head(plan, levels, timesteps, sums, gains, heads, latents)
    velocities = [velocity] + [plan.to_tensor(velocity, i) for i in range(1, tensors)]
    advanced = [plan.to_next_group(moved, i) for i in range(tensors)]
    return tuple(place(plan, velocities, advanced))


def solution(mesh):
    return jax.shard_map(
        local,
        mesh=mesh,
        in_specs=(
            P("section", "tensor"),
            P("section", "tensor"),
            P("section", "tensor"),
            P("section", None),
            P("tensor", None),
            P("tensor"),
            P("tensor", None),
            P(),
            P(),
            P(),
        ),
        out_specs=(P("section", None), P("section", None)),
        check_vma=False,
    )
```

```python
import functools
import math

import jax
import jax.numpy as jnp
from jax import lax
from jax.experimental import pallas as pl
from jax.experimental.pallas import tpu as pltpu
from jax.sharding import PartitionSpec as P

HD = 128
GROUPS = 8
MAX_HEAD_SPLIT = 4
NEG = -1e30
VMEM = pl.BlockSpec(memory_space=pltpu.VMEM)
ANY = pl.BlockSpec(memory_space=pl.ANY)
SMEM = pl.BlockSpec(memory_space=pltpu.SMEM)


def params(mib):
    return pltpu.CompilerParams(vmem_limit_bytes=mib * 1024 * 1024)


def struct(shape, dtype):
    return jax.ShapeDtypeStruct(shape, dtype)


class Plan:
    def __init__(self, queries):
        self.sections = lax.axis_size("section")
        self.tensors = lax.axis_size("tensor")
        self.rows, self.width = queries.shape
        self.heads = self.width // HD
        self.split = math.gcd(self.heads, MAX_HEAD_SPLIT)
        self.members = self.sections // self.split
        self.cols = self.width // self.split
        self.span = self.sections // GROUPS
        self.share = self.rows // self.tensors
        self.per = 2 if self.span % 2 == 0 and self.members % 2 == 0 else 1
        self.blocks = self.sections // self.per

    def part(self):
        return lax.axis_index("section") // self.members

    def to_part(self, value, step):
        pairs = [(s, s ^ (step * self.members)) for s in range(self.sections)]
        return lax.ppermute(value, "section", pairs)

    def to_member(self, value, step):
        return lax.ppermute(value, "section", [(s, s ^ step) for s in range(self.sections)])

    def to_tensor(self, value, step):
        return lax.ppermute(value, "tensor", [(t, t ^ step) for t in range(self.tensors)])

    def to_next_group(self, value, step):
        pairs = [
            (s * self.tensors + t, ((s + self.span) % self.sections) * self.tensors + (t ^ step))
            for s in range(self.sections)
            for t in range(self.tensors)
        ]
        return lax.ppermute(value, ("section", "tensor"), pairs)

    def gather_members(self, piece):
        pieces = {0: piece}
        step = self.members // 2
        while step:
            pieces.update({i ^ step: self.to_member(v, step) for i, v in list(pieces.items())})
            step //= 2
        return [pieces[i] for i in range(self.members)]


def pack(plan, step, *arrays):
    at = (plan.part() ^ step) * plan.cols
    return jnp.concatenate([lax.dynamic_slice_in_dim(a, at, plan.cols, 1) for a in arrays], axis=0)


def held(values, after):
    def kernel(*refs):
        pass

    return pl.pallas_call(
        kernel,
        out_shape=[struct(v.shape, v.dtype) for v in values],
        in_specs=[ANY] * (len(values) + len(after)),
        out_specs=[ANY] * len(values),
        input_output_aliases={i: i for i in range(len(values))},
        compiler_params=params(1),
    )(*values, *after)


def ready_kernel(plan, waits, order, gain, head_weight, *refs):
    shared, bias = refs[waits:]
    count = head_weight.shape[0]
    shared[pl.ds(0, count), :] = head_weight[...]
    rest, rows = gain[...], []
    for _ in range(3):
        rows.append(rest.astype(jnp.bfloat16))
        rest = rest - rows[-1].astype(jnp.float32)
    rows = [jnp.broadcast_to(row, (16, gain.shape[1])) for row in rows]
    shared[pl.ds(count, 48), :] = jnp.concatenate(rows, axis=0)
    me = lax.axis_index("section")

    def order_of(step, member):
        return order[(me ^ (step * plan.members + member)) // plan.span]

    for i in range(plan.split):
        for j in range(plan.blocks):
            first = j * plan.per
            seen = order_of(first // plan.members, first % plan.members) <= order_of(i, 0)
            bias[pl.ds(i * plan.blocks + j, 1), :] = jnp.full((1, HD), jnp.where(seen, 0.0, NEG))


def ready(plan, order, gain, head_weight, after):
    return pl.pallas_call(
        functools.partial(ready_kernel, plan, len(after)),
        out_shape=[
            struct((head_weight.shape[0] + 48, head_weight.shape[1]), jnp.bfloat16),
            struct((plan.split * plan.blocks, HD), jnp.float32),
        ],
        in_specs=[SMEM, VMEM, VMEM] + [ANY] * len(after),
        out_specs=[VMEM, VMEM],
        compiler_params=params(4),
    )(order, gain, head_weight, *after)


def attend_kernel(plan, steps, waits, bias, *refs):
    rows = plan.rows
    refs = refs[waits:]
    queries, refs = refs[: len(steps)], refs[len(steps) :]
    pieces, refs = refs[: plan.sections], refs[plan.sections :]
    outs, scores = refs[: len(steps)], refs[len(steps)]
    factor = math.log2(math.e) / math.sqrt(HD)
    many = len(steps) * rows
    width = plan.per * rows

    def hidden(j):
        at = [step * plan.blocks + j for step in steps]
        return jnp.concatenate([jnp.broadcast_to(bias[pl.ds(i, 1), :], (rows, HD)) for i in at], axis=0)

    def block(j, which, lanes):
        parts = pieces[j * plan.per : (j + 1) * plan.per]
        return jnp.concatenate([ref[pl.ds(which * rows, rows), lanes] for ref in parts], axis=0)

    for h in range(plan.cols // HD):
        lanes = pl.ds(h * HD, HD)
        q = [ref[pl.ds(ref.shape[0] - rows, rows), lanes] for ref in queries]
        q = jnp.concatenate(q, axis=0)
        top = None
        for j in range(plan.blocks):
            s = lax.dot_general(q, block(j, 0, lanes), (((1,), (1,)), ((), ())), preferred_element_type=jnp.float32)
            scores[:, pl.ds(j * width, width)] = s
            s = functools.reduce(jnp.maximum, [s[:, i : i + HD] for i in range(0, width, HD)])
            s = s + hidden(j)
            top = s if top is None else jnp.maximum(top, s)
        top = jnp.broadcast_to(jnp.max(top, axis=1, keepdims=True), top.shape)
        total = jnp.zeros((many, HD), jnp.float32)
        summed = jnp.zeros((many, HD), jnp.float32)
        for j in range(plan.blocks):
            base = top - hidden(j)
            w = [scores[:, pl.ds(j * width + i, HD)] for i in range(0, width, HD)]
            w = [jnp.exp2((s - base) * factor) for s in w]
            total += functools.reduce(jnp.add, w)
            w = jnp.concatenate(w, axis=1).astype(jnp.bfloat16)
            summed += jnp.dot(w, block(j, 1, lanes), preferred_element_type=jnp.float32)
        out = (summed / jnp.sum(total, axis=1, keepdims=True)).astype(jnp.bfloat16)
        for i, ref in enumerate(outs):
            ref[:, lanes] = out[i * rows : (i + 1) * rows]


def attend(plan, steps, bias, queries, pieces, after=()):
    keys = plan.sections * plan.rows
    return pl.pallas_call(
        functools.partial(attend_kernel, plan, steps, len(after)),
        out_shape=[struct((plan.rows, plan.cols), jnp.bfloat16)] * len(steps),
        in_specs=[VMEM] + [ANY] * len(after) + [VMEM] * (len(steps) + len(pieces)),
        out_specs=[VMEM] * len(steps),
        scratch_shapes=[pltpu.VMEM((len(steps) * plan.rows, keys), jnp.float32)],
        compiler_params=params(12),
        cost_estimate=pl.CostEstimate(
            flops=4 * len(steps) * plan.rows * keys * plan.cols,
            bytes_accessed=4 * keys * plan.cols,
            transcendentals=len(steps) * plan.rows * keys * plan.cols // HD,
        ),
    )(bias, *after, *queries, *pieces)


def project_kernel(plan, steps, begun, *refs):
    parts, weight, refs = refs[: len(steps)], refs[len(steps)], refs[len(steps) + 1 :]
    outs = refs[1:] if begun else refs
    part, tensor = plan.part(), lax.axis_index("tensor")
    tile = 512
    for at in range(0, weight.shape[1], tile):
        cols = pl.ds(at, tile)
        total = refs[0][:, cols] if begun else None
        for step, ref in zip(steps, parts):
            here = pl.ds(pl.multiple_of((part ^ step) * plan.cols, 128), plan.cols)
            term = jnp.dot(ref[...], weight[here, cols], preferred_element_type=jnp.float32)
            total = term if total is None else total + term
        if not begun:
            outs[0][:, cols] = total
        else:
            full = outs[-1]
            full[...] = total
            for step, out in enumerate(outs[:-1]):
                here = pl.ds(pl.multiple_of((tensor ^ step) * plan.share, 8), plan.share)
                out[:, cols] = full[here, :].astype(out.dtype)


def project(plan, steps, parts, weight, begun=None):
    width = weight.shape[1]
    if begun is None:
        shapes, scratch, extra = struct((plan.rows, width), jnp.float32), [], ()
    else:
        shapes = [struct((plan.share, width), jnp.float32)]
        shapes += [struct((plan.share, width), jnp.bfloat16)] * (plan.tensors - 1)
        scratch, extra = [pltpu.VMEM((plan.rows, 512), jnp.float32)], (begun,)
    return pl.pallas_call(
        functools.partial(project_kernel, plan, steps, begun is not None),
        out_shape=shapes,
        in_specs=[VMEM] * (len(parts) + 1 + len(extra)),
        out_specs=VMEM if begun is None else [VMEM] * plan.tensors,
        scratch_shapes=scratch,
        compiler_params=params(16),
        cost_estimate=pl.CostEstimate(flops=1, bytes_accessed=1, transcendentals=0),
    )(*parts, weight, *extra)


def head_kernel(plan, levels, timesteps, *refs):
    sums, refs = refs[: plan.tensors], refs[plan.tensors :]
    shared, refs = refs[: plan.tensors], refs[plan.tensors :]
    latents, velocity_ref, moved_ref, full, rows = refs
    tensor = lax.axis_index("tensor")
    total = sums[0][...]
    for ref in sums[1:]:
        total = total + ref[...].astype(jnp.float32)
    full[...] = total
    squares = jnp.sum(total * total, axis=1, keepdims=True)
    count = rows.shape[1]
    raw = None
    for step, ref in enumerate(shared):
        share = ref.shape[1]
        here = pl.ds(pl.multiple_of((tensor ^ step) * share, 128), share)
        gain = sum(ref[pl.ds(count + 16 * i, 16), :].astype(jnp.float32)[:1] for i in range(3))
        scaled = (full[:, here] * gain).astype(jnp.bfloat16)
        term = lax.dot_general(
            scaled,
            ref[pl.ds(0, count), :],
            (((1,), (1,)), ((), ())),
            preferred_element_type=jnp.float32,
        )
        raw = term if raw is None else raw + term
    rows[...] = raw * lax.rsqrt(squares / total.shape[1] + 1e-6)
    half = plan.share // 2
    velocity = jnp.concatenate(
        [rows[pl.ds(0, half, 2), :], rows[pl.ds(1, half, 2), :]], axis=1
    )
    level = levels[lax.axis_index("section") // plan.span]
    change = (timesteps[level + 1] - timesteps[level]).astype(jnp.float32)
    delta = jnp.full(velocity.shape, change, jnp.float32) / 1000.0
    velocity_ref[...] = velocity
    here = pl.ds(pl.multiple_of(tensor * half, 8), half)
    moved_ref[...] = latents[here, :] + delta * velocity


def head(plan, levels, timesteps, sums, shared, latents):
    half = struct((plan.share // 2, latents.shape[1]), jnp.float32)
    return pl.pallas_call(
        functools.partial(head_kernel, plan),
        out_shape=[half, half],
        in_specs=[SMEM, SMEM] + [VMEM] * (2 * plan.tensors + 1),
        out_specs=[VMEM, VMEM],
        scratch_shapes=[
            pltpu.VMEM(sums[0].shape, jnp.float32),
            pltpu.VMEM((plan.share, latents.shape[1] // 2), jnp.float32),
        ],
        compiler_params=params(12),
    )(levels, timesteps, *sums, *shared, latents)


def place_kernel(plan, *refs):
    velocities, moved = refs[: plan.tensors], refs[plan.tensors : 2 * plan.tensors]
    tensor = lax.axis_index("tensor")
    for parts, out in ((velocities, refs[-2]), (moved, refs[-1])):
        for step, ref in enumerate(parts):
            rows = ref.shape[0]
            out[pl.ds(pl.multiple_of((tensor ^ step) * rows, 8), rows), :] = ref[...]


def place(plan, velocities, moved):
    shape = struct((plan.rows // 2, velocities[0].shape[1]), jnp.float32)
    return pl.pallas_call(
        functools.partial(place_kernel, plan),
        out_shape=[shape, shape],
        in_specs=[VMEM] * (2 * plan.tensors),
        out_specs=[VMEM, VMEM],
        compiler_params=params(2),
    )(*velocities, *moved)


def local(queries, keys, values, latents, out_weight, gain, head_weight, levels, timesteps, order):
    plan = Plan(queries)
    split, tensors = plan.split, plan.tensors

    far, near = list(range(1, split)), [0]
    own, asked = pack(plan, 0, keys, values), [pack(plan, 0, queries)]
    if split == 4 and plan.members == 4:
        two = plan.to_part(pack(plan, 2, keys, values, queries), 2)
        one = plan.to_part(pack(plan, 1, keys, values, queries), 1)
        shared, bias = ready(plan, order, gain[None, :], head_weight.T, [one])
        own = plan.gather_members(own)
        ones = plan.gather_members(one[: 2 * plan.rows])
        three = pack(plan, 3, keys, values, queries)
        gate = [two, own[2]]
        three = plan.to_part(held([three], gate)[0] if gate else three, 3)
        asked += [one, two, three]
        twos = plan.gather_members(*held([two[: 2 * plan.rows]], [bias]))
        threes = plan.gather_members(*held([three[: 2 * plan.rows]], [ones[2], twos[2]]))
        pieces = own + ones + twos + threes
    else:
        shared, bias = ready(plan, order, gain[None, :], head_weight.T, [])
        sent = [own] + [plan.to_part(pack(plan, i, keys, values), i) for i in far]
        asked += [plan.to_part(pack(plan, i, queries), i) for i in far]
        pieces = [p for v in sent for p in plan.gather_members(v)]
    shared = [shared] + [plan.to_tensor(shared, i) for i in range(1, tensors)]

    attended = [None] * split
    done = []
    if far:
        done = attend(plan, far, bias, [asked[i] for i in far], pieces)
        attended[1:] = [plan.to_part(v, i) for i, v in zip(far, done)]
    (attended[0],) = attend(plan, near, bias, asked[:1], pieces, done[:1])
    sums = project(plan, near, attended[:1], out_weight)
    if far:
        attended[1:2] = held(attended[1:2], shared[1:])
    sums = project(plan, far, attended[1:], out_weight, sums)
    sums = [sums[0]] + [plan.to_tensor(sums[i], i) for i in range(1, tensors)]
    velocity, moved = head(plan, levels, timesteps, sums, shared, latents)
    advanced = [plan.to_next_group(moved, i) for i in range(tensors)]
    velocities = [velocity] + [plan.to_tensor(velocity, i) for i in range(1, tensors)]
    return place(plan, advanced, velocities)[::-1]


def solution(mesh):
    return jax.shard_map(
        local,
        mesh=mesh,
        in_specs=(
            P("section", "tensor"),
            P("section", "tensor"),
            P("section", "tensor"),
            P("section", None),
            P("tensor", None),
            P("tensor"),
            P("tensor", None),
            P(),
            P(),
            P(),
        ),
        out_specs=(P("section", None), P("section", None)),
        check_vma=False,
    )
```

```python
import functools
import math

import jax
import jax.numpy as jnp
from jax import lax
from jax.experimental import pallas as pl
from jax.experimental.pallas import tpu as pltpu
from jax.sharding import PartitionSpec as P

HD = 128
GROUPS = 8
MAX_HEAD_SPLIT = 4
NEG = -1e30
VMEM = pl.BlockSpec(memory_space=pltpu.VMEM)
ANY = pl.BlockSpec(memory_space=pl.ANY)
SMEM = pl.BlockSpec(memory_space=pltpu.SMEM)


def params(mib):
    return pltpu.CompilerParams(vmem_limit_bytes=mib * 1024 * 1024)


def struct(shape, dtype):
    return jax.ShapeDtypeStruct(shape, dtype)


class Plan:
    def __init__(self, queries):
        self.sections = lax.axis_size("section")
        self.tensors = lax.axis_size("tensor")
        self.rows, self.width = queries.shape
        self.heads = self.width // HD
        self.split = math.gcd(self.heads, MAX_HEAD_SPLIT)
        self.members = self.sections // self.split
        self.cols = self.width // self.split
        self.span = self.sections // GROUPS
        self.share = self.rows // self.tensors
        self.per = 2 if self.span % 2 == 0 and self.members % 2 == 0 else 1
        self.blocks = self.sections // self.per

    def row_starts(self):
        tensor = lax.axis_index("tensor")
        return [(tensor ^ step) * self.share for step in [*range(1, self.tensors), 0]]

    def part(self):
        return lax.axis_index("section") // self.members

    def to_part(self, value, step):
        pairs = [(s, s ^ (step * self.members)) for s in range(self.sections)]
        return lax.ppermute(value, "section", pairs)

    def to_member(self, value, step):
        return lax.ppermute(value, "section", [(s, s ^ step) for s in range(self.sections)])

    def to_tensor(self, value, step):
        return lax.ppermute(value, "tensor", [(t, t ^ step) for t in range(self.tensors)])

    def to_next_group(self, value, step):
        pairs = [
            (s * self.tensors + t, ((s + self.span) % self.sections) * self.tensors + (t ^ step))
            for s in range(self.sections)
            for t in range(self.tensors)
        ]
        return lax.ppermute(value, ("section", "tensor"), pairs)

    def gather_members(self, piece):
        pieces = {0: piece}
        step = self.members // 2
        while step:
            pieces.update({i ^ step: self.to_member(v, step) for i, v in list(pieces.items())})
            step //= 2
        return [pieces[i] for i in range(self.members)]


def pack(plan, step, *arrays):
    at = (plan.part() ^ step) * plan.cols
    return jnp.concatenate([lax.dynamic_slice_in_dim(a, at, plan.cols, 1) for a in arrays], axis=0)


def held(values, after):
    def kernel(*refs):
        pass

    return pl.pallas_call(
        kernel,
        out_shape=[struct(v.shape, v.dtype) for v in values],
        in_specs=[ANY] * (len(values) + len(after)),
        out_specs=[ANY] * len(values),
        input_output_aliases={i: i for i in range(len(values))},
        compiler_params=params(1),
    )(*values, *after)


def ready_kernel(plan, waits, order, gain, head_weight, *refs):
    shared, bias = refs[waits:]
    count = head_weight.shape[0]
    shared[pl.ds(0, count), :] = head_weight[...]
    rest, rows = gain[...], []
    for _ in range(3):
        rows.append(rest.astype(jnp.bfloat16))
        rest = rest - rows[-1].astype(jnp.float32)
    rows = [jnp.broadcast_to(row, (16, gain.shape[1])) for row in rows]
    shared[pl.ds(count, 48), :] = jnp.concatenate(rows, axis=0)
    me = lax.axis_index("section")

    def order_of(step, member):
        return order[(me ^ (step * plan.members + member)) // plan.span]

    for i in range(plan.split):
        for j in range(plan.blocks):
            first = j * plan.per
            seen = order_of(first // plan.members, first % plan.members) <= order_of(i, 0)
            bias[pl.ds(i * plan.blocks + j, 1), :] = jnp.full((1, HD), jnp.where(seen, 0.0, NEG))


def ready(plan, order, gain, head_weight, after):
    return pl.pallas_call(
        functools.partial(ready_kernel, plan, len(after)),
        out_shape=[
            struct((head_weight.shape[0] + 48, head_weight.shape[1]), jnp.bfloat16),
            struct((plan.split * plan.blocks, HD), jnp.float32),
        ],
        in_specs=[SMEM, VMEM, VMEM] + [ANY] * len(after),
        out_specs=[VMEM, VMEM],
        compiler_params=params(4),
    )(order, gain, head_weight, *after)


def attend_kernel(plan, blocks, begun, last, bias, *refs):
    rows = plan.rows
    before, refs = (refs[:3], refs[3:]) if begun else (None, refs)
    queries, refs = refs[: plan.split], refs[plan.split :]
    pieces, refs = refs[: len(blocks) * plan.per], refs[len(blocks) * plan.per :]
    outs, scores = refs[:-1], refs[-1]
    factor = math.log2(math.e) / math.sqrt(HD)
    width = plan.per * rows

    def hidden(j):
        at = [step * plan.blocks + j for step in range(plan.split)]
        return jnp.concatenate([jnp.broadcast_to(bias[pl.ds(i, 1), :], (rows, HD)) for i in at], axis=0)

    def block(at, which, lanes):
        parts = pieces[at * plan.per : (at + 1) * plan.per]
        return jnp.concatenate([ref[pl.ds(which * rows, rows), lanes] for ref in parts], axis=0)

    for h in range(plan.cols // HD):
        lanes = pl.ds(h * HD, HD)
        q = [
            ref[pl.ds(pl.multiple_of(ref.shape[0] - rows + start, 16), plan.share), lanes]
            for ref in queries
            for start in plan.row_starts()
        ]
        q = jnp.concatenate(q, axis=0)
        top = before[0][h] if begun else None
        for at, j in enumerate(blocks):
            s = lax.dot_general(q, block(at, 0, lanes), (((1,), (1,)), ((), ())), preferred_element_type=jnp.float32)
            scores[:, pl.ds(at * width, width)] = s
            s = functools.reduce(jnp.maximum, [s[:, i : i + HD] for i in range(0, width, HD)])
            s = s + hidden(j)
            top = s if top is None else jnp.maximum(top, s)
        top = jnp.broadcast_to(jnp.max(top, axis=1, keepdims=True), top.shape)
        if begun:
            kept = jnp.exp2((before[0][h] - top) * factor)
            total, summed = kept * before[1][h], kept * before[2][h]
        else:
            total = summed = jnp.zeros(top.shape, jnp.float32)
        for at, j in enumerate(blocks):
            base = top - hidden(j)
            w = [scores[:, pl.ds(at * width + i, HD)] for i in range(0, width, HD)]
            w = [jnp.exp2((s - base) * factor) for s in w]
            total += functools.reduce(jnp.add, w)
            w = jnp.concatenate(w, axis=1).astype(jnp.bfloat16)
            summed += jnp.dot(w, block(at, 1, lanes), preferred_element_type=jnp.float32)
        if last:
            out = (summed / jnp.sum(total, axis=1, keepdims=True)).astype(jnp.bfloat16)
            others = rows - plan.share
            for i, (away, kept) in enumerate(zip(outs[: plan.split], outs[plan.split :])):
                away[:, lanes] = out[i * rows : i * rows + others]
                kept[:, lanes] = out[i * rows + others : (i + 1) * rows]
        else:
            outs[0][h], outs[1][h], outs[2][h] = top, total, summed


def attend(plan, blocks, bias, queries, pieces, state=(), last=False):
    many = plan.split * plan.rows
    shapes = [struct((plan.cols // HD, many, HD), jnp.float32)] * 3
    if last:
        shapes = [struct((plan.rows - plan.share, plan.cols), jnp.bfloat16)] * plan.split
        shapes += [struct((plan.share, plan.cols), jnp.bfloat16)] * plan.split
    pieces = [p for j in blocks for p in pieces[j]]
    out = pl.pallas_call(
        functools.partial(attend_kernel, plan, blocks, bool(state), last),
        out_shape=shapes,
        in_specs=[VMEM] * (1 + len(state) + plan.split + len(pieces)),
        out_specs=[VMEM] * len(shapes),
        scratch_shapes=[pltpu.VMEM((many, len(pieces) * plan.rows), jnp.float32)],
        compiler_params=params(12),
        cost_estimate=pl.CostEstimate(
            flops=16 * many * len(pieces) * plan.rows * plan.cols, bytes_accessed=0, transcendentals=0
        ),
    )(bias, *state, *queries, *pieces)
    return list(out)


def project_kernel(plan, steps, begun, *refs):
    count = len(steps)
    parts, weight, refs = refs[:count], refs[count], refs[count + 1 :]
    outs = refs[1:] if begun else refs
    tile = 512
    for at in range(0, weight.shape[1], tile):
        cols = pl.ds(at, tile)
        total = refs[0][:, cols] if begun else 0.0
        for step, ref in zip(steps, parts):
            here = pl.ds(pl.multiple_of((plan.part() ^ step) * plan.cols, 128), plan.cols)
            total += jnp.dot(ref[...], weight[here, cols], preferred_element_type=jnp.float32)
        rows = total.shape[0] // len(outs)
        for i, out in enumerate(outs):
            out[:, cols] = total[i * rows : (i + 1) * rows].astype(out.dtype)


def project(plan, steps, parts, weight, begun=None, split=False):
    rows, width = parts[0].shape[0], weight.shape[1]
    extra = () if begun is None else (begun,)
    shapes = [struct((rows, width), jnp.float32)]
    if split:
        shapes = [struct((plan.share, width), jnp.bfloat16)] * (rows // plan.share)
    out = pl.pallas_call(
        functools.partial(project_kernel, plan, steps, bool(extra)),
        out_shape=shapes,
        in_specs=[VMEM] * (len(parts) + 1 + len(extra)),
        out_specs=[VMEM] * len(shapes),
        compiler_params=params(8),
        cost_estimate=pl.CostEstimate(flops=0, bytes_accessed=0, transcendentals=0),
    )(*parts, weight, *extra)
    return list(out) if split else out[0]


def head_kernel(plan, levels, timesteps, *refs):
    sums, refs = refs[: plan.tensors], refs[plan.tensors :]
    shared, refs = refs[: plan.tensors], refs[plan.tensors :]
    latents, velocity_ref, moved_ref, full, rows = refs
    tensor = lax.axis_index("tensor")
    total = sums[0][...]
    for ref in sums[1:]:
        total = total + ref[...].astype(jnp.float32)
    full[...] = total
    squares = jnp.sum(total * total, axis=1, keepdims=True)
    count = rows.shape[1]
    raw = None
    for step, ref in enumerate(shared):
        share = ref.shape[1]
        here = pl.ds(pl.multiple_of((tensor ^ step) * share, 128), share)
        gain = sum(ref[pl.ds(count + 16 * i, 16), :].astype(jnp.float32)[:1] for i in range(3))
        scaled = (full[:, here] * gain).astype(jnp.bfloat16)
        term = lax.dot_general(
            scaled,
            ref[pl.ds(0, count), :],
            (((1,), (1,)), ((), ())),
            preferred_element_type=jnp.float32,
        )
        raw = term if raw is None else raw + term
    rows[...] = raw * lax.rsqrt(squares / total.shape[1] + 1e-6)
    half = plan.share // 2
    velocity = jnp.concatenate(
        [rows[pl.ds(0, half, 2), :], rows[pl.ds(1, half, 2), :]], axis=1
    )
    level = levels[lax.axis_index("section") // plan.span]
    change = (timesteps[level + 1] - timesteps[level]).astype(jnp.float32)
    delta = jnp.full(velocity.shape, change, jnp.float32) / 1000.0
    velocity_ref[...] = velocity
    here = pl.ds(pl.multiple_of(tensor * half, 8), half)
    moved_ref[...] = latents[here, :] + delta * velocity


def head(plan, levels, timesteps, sums, shared, latents):
    half = struct((plan.share // 2, latents.shape[1]), jnp.float32)
    return pl.pallas_call(
        functools.partial(head_kernel, plan),
        out_shape=[half, half],
        in_specs=[SMEM, SMEM] + [VMEM] * (2 * plan.tensors + 1),
        out_specs=[VMEM, VMEM],
        scratch_shapes=[
            pltpu.VMEM(sums[0].shape, jnp.float32),
            pltpu.VMEM((plan.share, latents.shape[1] // 2), jnp.float32),
        ],
        compiler_params=params(12),
    )(levels, timesteps, *sums, *shared, latents)


def place_kernel(plan, *refs):
    velocities, moved = refs[: plan.tensors], refs[plan.tensors : 2 * plan.tensors]
    tensor = lax.axis_index("tensor")
    for parts, out in ((velocities, refs[-2]), (moved, refs[-1])):
        for step, ref in enumerate(parts):
            rows = ref.shape[0]
            out[pl.ds(pl.multiple_of((tensor ^ step) * rows, 8), rows), :] = ref[...]


def place(plan, velocities, moved):
    shape = struct((plan.rows // 2, velocities[0].shape[1]), jnp.float32)
    return pl.pallas_call(
        functools.partial(place_kernel, plan),
        out_shape=[shape, shape],
        in_specs=[VMEM] * (2 * plan.tensors),
        out_specs=[VMEM, VMEM],
        compiler_params=params(2),
    )(*velocities, *moved)


def local(queries, keys, values, latents, out_weight, gain, head_weight, levels, timesteps, order):
    plan = Plan(queries)
    split, tensors = plan.split, plan.tensors

    far, near = list(range(1, split)), [0]
    own, asked = pack(plan, 0, keys, values), [pack(plan, 0, queries)]
    if split == 4 and plan.members == 4:
        two = plan.to_part(pack(plan, 2, keys, values, queries), 2)
        one = plan.to_part(pack(plan, 1, keys, values, queries), 1)
        own = plan.gather_members(own)
        shared, bias = ready(plan, order, gain[None, :], head_weight.T, [own[2]])
        shared = [shared] + [plan.to_tensor(shared, i) for i in range(1, tensors)]
        ones = plan.gather_members(one[: 2 * plan.rows])
        (three,) = held([pack(plan, 3, keys, values, queries)], [two, own[2], bias])
        three = plan.to_part(three, 3)
        asked += [one, two, three]
        twos = plan.gather_members(*held([two[: 2 * plan.rows]], []))
        threes = [*held([three[: 2 * plan.rows]], [ones[2], twos[2]])]
        threes += [plan.to_member(threes[0], i) for i in (1, 2)]
        pairs = [v[i : i + 2] for v in (own, ones, twos) for i in (0, 2)]
        pairs.append(threes[:2])
        state = attend(plan, [0, 2, 4, 6, 1, 3], bias, asked, pairs)
        (last,) = held(threes[2:], [state[0]])
        pairs.append([last, plan.to_member(last, 1)])
        attended = attend(plan, [5, 7], bias, asked, pairs, state, True)
    else:
        shared, bias = ready(plan, order, gain[None, :], head_weight.T, [])
        shared = [shared] + [plan.to_tensor(shared, i) for i in range(1, tensors)]
        sent = [own] + [plan.to_part(pack(plan, i, keys, values), i) for i in far]
        asked += [plan.to_part(pack(plan, i, queries), i) for i in far]
        pieces = [p for v in sent for p in plan.gather_members(v)]
        pairs = [pieces[i : i + plan.per] for i in range(0, len(pieces), plan.per)]
        blocks = list(range(plan.blocks))
        own_blocks = blocks[:: plan.blocks // split]
        state = attend(plan, own_blocks, bias, asked, pairs)
        attended = attend(plan, [j for j in blocks if j not in own_blocks], bias, asked, pairs, state, True)

    away, kept = attended[:split], attended[split:]
    away = [plan.to_part(v, i) if i else v for i, v in enumerate(away)]
    rest = far or near
    begun = project(plan, near, away[:1], out_weight) if far else None
    away[-1:] = held(away[-1:], shared[1:])
    away = project(plan, rest, [away[i] for i in rest], out_weight, begun, True)
    away = [plan.to_tensor(v, i + 1) for i, v in enumerate(away)]
    kept = [plan.to_part(v, i) if i else v for i, v in enumerate(kept)]
    begun = project(plan, near, kept[:1], out_weight) if far else None
    sums = [project(plan, rest, [kept[i] for i in rest], out_weight, begun), *away]
    velocity, moved = head(plan, levels, timesteps, sums, shared, latents)
    advanced = [plan.to_next_group(moved, i) for i in range(tensors)]
    velocities = [velocity] + [plan.to_tensor(velocity, i) for i in range(1, tensors)]
    return place(plan, advanced, velocities)[::-1]


def solution(mesh):
    return jax.shard_map(
        local,
        mesh=mesh,
        in_specs=(
            P("section", "tensor"),
            P("section", "tensor"),
            P("section", "tensor"),
            P("section", None),
            P("tensor", None),
            P("tensor"),
            P("tensor", None),
            P(),
            P(),
            P(),
        ),
        out_specs=(P("section", None), P("section", None)),
        check_vma=False,
    )
```

```python
import functools
import math

import jax
import jax.numpy as jnp
from jax import lax
from jax.experimental import pallas as pl
from jax.experimental.pallas import tpu as pltpu
from jax.sharding import PartitionSpec as P

HD = 128
GROUPS = 8
MAX_HEAD_SPLIT = 4
NEG = -1e30
VMEM = pl.BlockSpec(memory_space=pltpu.VMEM)
ANY = pl.BlockSpec(memory_space=pl.ANY)
SMEM = pl.BlockSpec(memory_space=pltpu.SMEM)


def params(mib):
    return pltpu.CompilerParams(vmem_limit_bytes=mib * 1024 * 1024)


def struct(shape, dtype):
    return jax.ShapeDtypeStruct(shape, dtype)


class Plan:
    def __init__(self, queries):
        self.sections = lax.axis_size("section")
        self.tensors = lax.axis_size("tensor")
        self.rows, self.width = queries.shape
        self.heads = self.width // HD
        self.split = math.gcd(self.heads, MAX_HEAD_SPLIT)
        self.members = self.sections // self.split
        self.cols = self.width // self.split
        self.span = self.sections // GROUPS
        self.share = self.rows // self.tensors
        self.per = 2 if self.span % 2 == 0 and self.members % 2 == 0 else 1
        self.blocks = self.sections // self.per

    def row_starts(self):
        tensor = lax.axis_index("tensor")
        return [(tensor ^ step) * self.share for step in [*range(1, self.tensors), 0]]

    def part(self):
        return lax.axis_index("section") // self.members

    def to_part(self, value, step):
        pairs = [(s, s ^ (step * self.members)) for s in range(self.sections)]
        return lax.ppermute(value, "section", pairs)

    def to_member(self, value, step):
        return lax.ppermute(value, "section", [(s, s ^ step) for s in range(self.sections)])

    def to_tensor(self, value, step):
        return lax.ppermute(value, "tensor", [(t, t ^ step) for t in range(self.tensors)])

    def to_next_group(self, value, step):
        pairs = [
            (s * self.tensors + t, ((s + self.span) % self.sections) * self.tensors + (t ^ step))
            for s in range(self.sections)
            for t in range(self.tensors)
        ]
        return lax.ppermute(value, ("section", "tensor"), pairs)

    def gather_members(self, piece):
        pieces = {0: piece}
        step = self.members // 2
        while step:
            pieces.update({i ^ step: self.to_member(v, step) for i, v in list(pieces.items())})
            step //= 2
        return [pieces[i] for i in range(self.members)]


def pack(plan, step, *arrays):
    at = (plan.part() ^ step) * plan.cols
    return jnp.concatenate([lax.dynamic_slice_in_dim(a, at, plan.cols, 1) for a in arrays], axis=0)


def pack_late_kernel(plan, steps, waits, *refs):
    sources, refs = refs[:3], refs[3 + waits :]
    for step, ref in zip(steps, refs):
        here = pl.ds(pl.multiple_of((plan.part() ^ step) * plan.cols, 128), plan.cols)
        rows = [source[:, here] for source in sources]
        ref[...] = jnp.concatenate(rows, axis=0)[3 * plan.rows - ref.shape[0] :]


def pack_late(plan, steps, arrays, after):
    rows = [(3 if step else 1) * plan.rows for step in steps]
    return pl.pallas_call(
        functools.partial(pack_late_kernel, plan, steps, len(after)),
        out_shape=[struct((n, plan.cols), arrays[0].dtype) for n in rows],
        in_specs=[VMEM] * 3 + [ANY] * len(after),
        out_specs=[VMEM] * len(steps),
        compiler_params=params(4),
    )(*arrays, *after)


def held(values, after):
    def kernel(*refs):
        pass

    return pl.pallas_call(
        kernel,
        out_shape=[struct(v.shape, v.dtype) for v in values],
        in_specs=[ANY] * (len(values) + len(after)),
        out_specs=[ANY] * len(values),
        input_output_aliases={i: i for i in range(len(values))},
        compiler_params=params(1),
    )(*values, *after)


def ready_kernel(plan, waits, order, levels, timesteps, gain, head_weight, *refs):
    shared, bias, delta = refs[waits:]
    count = head_weight.shape[0]
    shared[pl.ds(0, count), :] = head_weight[...]
    rest, rows = gain[...], []
    for _ in range(3):
        rows.append(rest.astype(jnp.bfloat16))
        rest = rest - rows[-1].astype(jnp.float32)
    rows = [jnp.broadcast_to(row, (16, gain.shape[1])) for row in rows]
    shared[pl.ds(count, 48), :] = jnp.concatenate(rows, axis=0)
    me = lax.axis_index("section")
    level = levels[me // plan.span]
    change = (timesteps[level + 1] - timesteps[level]).astype(jnp.float32)
    delta[...] = jnp.full(delta.shape, change, jnp.float32) / 1000.0

    def order_of(step, member):
        return order[(me ^ (step * plan.members + member)) // plan.span]

    for i in range(plan.split):
        for j in range(plan.blocks):
            first = j * plan.per
            seen = order_of(first // plan.members, first % plan.members) <= order_of(i, 0)
            bias[pl.ds(i * plan.blocks + j, 1), :] = jnp.full((1, HD), jnp.where(seen, 0.0, NEG))


def ready(plan, order, levels, timesteps, gain, head_weight, after):
    return pl.pallas_call(
        functools.partial(ready_kernel, plan, len(after)),
        out_shape=[
            struct((head_weight.shape[0] + 48, head_weight.shape[1]), jnp.bfloat16),
            struct((plan.split * plan.blocks, HD), jnp.float32),
            struct((8, HD), jnp.float32),
        ],
        in_specs=[SMEM] * 3 + [VMEM] * 2 + [ANY] * len(after),
        out_specs=[VMEM] * 3,
        compiler_params=params(4),
    )(order, levels, timesteps, gain, head_weight, *after)


def attend_kernel(plan, blocks, begun, last, bias, *refs):
    rows = plan.rows
    before, refs = (refs[:3], refs[3:]) if begun else (None, refs)
    queries, refs = refs[: plan.split], refs[plan.split :]
    pieces, refs = refs[: len(blocks) * plan.per], refs[len(blocks) * plan.per :]
    outs, scores = refs[:-1], refs[-1]
    factor = math.log2(math.e) / math.sqrt(HD)
    width = plan.per * rows

    def hidden(j):
        at = [step * plan.blocks + j for step in range(plan.split)]
        return jnp.concatenate([jnp.broadcast_to(bias[pl.ds(i, 1), :], (rows, HD)) for i in at], axis=0)

    def block(at, which, lanes):
        parts = pieces[at * plan.per : (at + 1) * plan.per]
        return jnp.concatenate([ref[pl.ds(which * rows, rows), lanes] for ref in parts], axis=0)

    for h in range(plan.cols // HD):
        lanes = pl.ds(h * HD, HD)
        q = [
            ref[pl.ds(pl.multiple_of(ref.shape[0] - rows + start, 16), plan.share), lanes]
            for ref in queries
            for start in plan.row_starts()
        ]
        q = jnp.concatenate(q, axis=0)
        top = before[0][h] if begun else None
        for at, j in enumerate(blocks):
            s = lax.dot_general(q, block(at, 0, lanes), (((1,), (1,)), ((), ())), preferred_element_type=jnp.float32)
            scores[:, pl.ds(at * width, width)] = s
            s = functools.reduce(jnp.maximum, [s[:, i : i + HD] for i in range(0, width, HD)])
            s = s + hidden(j)
            top = s if top is None else jnp.maximum(top, s)
        top = jnp.broadcast_to(jnp.max(top, axis=1, keepdims=True), top.shape)
        if begun:
            kept = jnp.exp2((before[0][h] - top) * factor)
            total, summed = kept * before[1][h], kept * before[2][h]
        else:
            total = summed = jnp.zeros(top.shape, jnp.float32)
        for at, j in enumerate(blocks):
            base = top - hidden(j)
            w = [scores[:, pl.ds(at * width + i, HD)] for i in range(0, width, HD)]
            w = [jnp.exp2((s - base) * factor) for s in w]
            total += functools.reduce(jnp.add, w)
            w = jnp.concatenate(w, axis=1).astype(jnp.bfloat16)
            summed += jnp.dot(w, block(at, 1, lanes), preferred_element_type=jnp.float32)
        if last:
            out = (summed / jnp.sum(total, axis=1, keepdims=True)).astype(jnp.bfloat16)
            others = rows - plan.share
            for i, (away, kept) in enumerate(zip(outs[: plan.split], outs[plan.split :])):
                away[:, lanes] = out[i * rows : i * rows + others]
                kept[:, lanes] = out[i * rows + others : (i + 1) * rows]
        else:
            outs[0][h], outs[1][h], outs[2][h] = top, total, summed


def attend(plan, blocks, bias, queries, pieces, state=(), last=False):
    many = plan.split * plan.rows
    shapes = [struct((plan.cols // HD, many, HD), jnp.float32)] * 3
    if last:
        shapes = [struct((plan.rows - plan.share, plan.cols), jnp.bfloat16)] * plan.split
        shapes += [struct((plan.share, plan.cols), jnp.bfloat16)] * plan.split
    pieces = [p for j in blocks for p in pieces[j]]
    out = pl.pallas_call(
        functools.partial(attend_kernel, plan, blocks, bool(state), last),
        out_shape=shapes,
        in_specs=[VMEM] * (1 + len(state) + plan.split + len(pieces)),
        out_specs=[VMEM] * len(shapes),
        scratch_shapes=[pltpu.VMEM((many, len(pieces) * plan.rows), jnp.float32)],
        compiler_params=params(12),
        cost_estimate=pl.CostEstimate(
            flops=16 * many * len(pieces) * plan.rows * plan.cols, bytes_accessed=0, transcendentals=0
        ),
    )(bias, *state, *queries, *pieces)
    return list(out)


def project_kernel(plan, steps, begun, *refs):
    count = len(steps)
    parts, weight, refs = refs[:count], refs[count], refs[count + 1 :]
    outs = refs[1:] if begun else refs
    tile = 512
    for at in range(0, weight.shape[1], tile):
        cols = pl.ds(at, tile)
        total = refs[0][:, cols] if begun else 0.0
        for step, ref in zip(steps, parts):
            here = pl.ds(pl.multiple_of((plan.part() ^ step) * plan.cols, 128), plan.cols)
            total += jnp.dot(ref[...], weight[here, cols], preferred_element_type=jnp.float32)
        rows = total.shape[0] // len(outs)
        for i, out in enumerate(outs):
            out[:, cols] = total[i * rows : (i + 1) * rows].astype(out.dtype)


def project(plan, steps, parts, weight, begun=None, split=False):
    rows, width = parts[0].shape[0], weight.shape[1]
    extra = () if begun is None else (begun,)
    shapes = [struct((rows, width), jnp.float32)]
    if split:
        shapes = [struct((plan.share, width), jnp.bfloat16)] * (rows // plan.share)
    out = pl.pallas_call(
        functools.partial(project_kernel, plan, steps, bool(extra)),
        out_shape=shapes,
        in_specs=[VMEM] * (len(parts) + 1 + len(extra)),
        out_specs=[VMEM] * len(shapes),
        compiler_params=params(8),
        cost_estimate=pl.CostEstimate(flops=0, bytes_accessed=0, transcendentals=0),
    )(*parts, weight, *extra)
    return list(out) if split else out[0]


def head_kernel(plan, delta, *refs):
    sums, refs = refs[: plan.tensors], refs[plan.tensors :]
    shared, refs = refs[: plan.tensors], refs[plan.tensors :]
    latents, velocity_ref, moved_ref, full, rows = refs
    tensor = lax.axis_index("tensor")
    total = sums[0][...]
    for ref in sums[1:]:
        total = total + ref[...].astype(jnp.float32)
    full[...] = total
    squares = jnp.sum(total * total, axis=1, keepdims=True)
    count = rows.shape[1]
    raw = None
    for step, ref in enumerate(shared):
        share = ref.shape[1]
        here = pl.ds(pl.multiple_of((tensor ^ step) * share, 128), share)
        gain = sum(ref[pl.ds(count + 16 * i, 16), :].astype(jnp.float32)[:1] for i in range(3))
        scaled = (full[:, here] * gain).astype(jnp.bfloat16)
        term = lax.dot_general(
            scaled,
            ref[pl.ds(0, count), :],
            (((1,), (1,)), ((), ())),
            preferred_element_type=jnp.float32,
        )
        raw = term if raw is None else raw + term
    rows[...] = raw * lax.rsqrt(squares / total.shape[1] + 1e-6)
    half = plan.share // 2
    velocity = jnp.concatenate(
        [rows[pl.ds(0, half, 2), :], rows[pl.ds(1, half, 2), :]], axis=1
    )
    velocity_ref[...] = velocity
    here = pl.ds(pl.multiple_of(tensor * half, 8), half)
    moved_ref[...] = latents[here, :] + delta[pl.ds(0, 1), :] * velocity


def head(plan, delta, sums, shared, latents):
    half = struct((plan.share // 2, latents.shape[1]), jnp.float32)
    return pl.pallas_call(
        functools.partial(head_kernel, plan),
        out_shape=[half, half],
        in_specs=[VMEM] * (2 * plan.tensors + 2),
        out_specs=[VMEM, VMEM],
        scratch_shapes=[
            pltpu.VMEM(sums[0].shape, jnp.float32),
            pltpu.VMEM((plan.share, latents.shape[1] // 2), jnp.float32),
        ],
        compiler_params=params(12),
    )(delta, *sums, *shared, latents)


def place_kernel(plan, *refs):
    velocities, moved = refs[: plan.tensors], refs[plan.tensors : 2 * plan.tensors]
    tensor = lax.axis_index("tensor")
    for parts, out in ((velocities, refs[-2]), (moved, refs[-1])):
        for step, ref in enumerate(parts):
            rows = ref.shape[0]
            out[pl.ds(pl.multiple_of((tensor ^ step) * rows, 8), rows), :] = ref[...]


def place(plan, velocities, moved):
    shape = struct((plan.rows // 2, velocities[0].shape[1]), jnp.float32)
    return pl.pallas_call(
        functools.partial(place_kernel, plan),
        out_shape=[shape, shape],
        in_specs=[VMEM] * (2 * plan.tensors),
        out_specs=[VMEM, VMEM],
        compiler_params=params(2),
    )(*velocities, *moved)


def local(queries, keys, values, latents, out_weight, gain, head_weight, levels, timesteps, order):
    plan = Plan(queries)
    split, tensors = plan.split, plan.tensors

    far, near = list(range(1, split)), [0]
    own = pack(plan, 0, keys, values)
    if split == 4 and plan.members == 4:
        two = plan.to_part(pack(plan, 2, keys, values, queries), 2)
        one = plan.to_part(pack(plan, 1, keys, values, queries), 1)
        own = plan.gather_members(own)
        late, *asked = pack_late(plan, [3, 0], (keys, values, queries), [own[2]])
        shared, bias, delta = ready(plan, order, levels, timesteps, gain[None, :], head_weight.T, [own[2], late])
        shared = [shared] + [plan.to_tensor(shared, i) for i in range(1, tensors)]
        ones = plan.gather_members(one[: 2 * plan.rows])
        (three,) = held([late], [two, own[2], bias])
        three = plan.to_part(three, 3)
        asked += [one, two, three]
        twos = plan.gather_members(*held([two[: 2 * plan.rows]], []))
        threes = [*held([three[: 2 * plan.rows]], [ones[2], twos[2], *shared[1:]])]
        threes += [plan.to_member(threes[0], i) for i in (1, 2)]
        pairs = [v[i : i + 2] for v in (own, ones, twos) for i in (0, 2)]
        pairs.append(threes[:2])
        state = attend(plan, [0, 2, 4, 6, 1, 3, 5], bias, asked, pairs)
        (last,) = held(threes[2:], [state[0]])
        pairs.append([last, plan.to_member(last, 1)])
        attended = attend(plan, [7], bias, asked, pairs, state, True)
    else:
        shared, bias, delta = ready(plan, order, levels, timesteps, gain[None, :], head_weight.T, [])
        shared = [shared] + [plan.to_tensor(shared, i) for i in range(1, tensors)]
        sent = [own] + [plan.to_part(pack(plan, i, keys, values), i) for i in far]
        asked = [pack(plan, 0, queries)] + [plan.to_part(pack(plan, i, queries), i) for i in far]
        pieces = [p for v in sent for p in plan.gather_members(v)]
        pairs = [pieces[i : i + plan.per] for i in range(0, len(pieces), plan.per)]
        blocks = list(range(plan.blocks))
        own_blocks = blocks[:: plan.blocks // split]
        state = attend(plan, own_blocks, bias, asked, pairs)
        attended = attend(plan, [j for j in blocks if j not in own_blocks], bias, asked, pairs, state, True)

    away, kept = attended[:split], attended[split:]
    away = [plan.to_part(v, i) if i else v for i, v in enumerate(away)]
    rest = far or near
    begun = project(plan, near, away[:1], out_weight) if far else None
    away = project(plan, rest, [away[i] for i in rest], out_weight, begun, True)
    away = [plan.to_tensor(v, i + 1) for i, v in enumerate(away)]
    kept = [plan.to_part(v, i) if i else v for i, v in enumerate(kept)]
    begun = project(plan, near, kept[:1], out_weight) if far else None
    sums = [project(plan, rest, [kept[i] for i in rest], out_weight, begun), *away]
    velocity, moved = head(plan, delta, sums, shared, latents)
    advanced = [plan.to_next_group(moved, i) for i in range(tensors)]
    velocities = [velocity] + [plan.to_tensor(velocity, i) for i in range(1, tensors)]
    return place(plan, advanced, velocities)[::-1]


def solution(mesh):
    return jax.shard_map(
        local,
        mesh=mesh,
        in_specs=(
            P("section", "tensor"),
            P("section", "tensor"),
            P("section", "tensor"),
            P("section", None),
            P("tensor", None),
            P("tensor"),
            P("tensor", None),
            P(),
            P(),
            P(),
        ),
        out_specs=(P("section", None), P("section", None)),
        check_vma=False,
    )
```

```python
import functools
import math

import jax
import jax.numpy as jnp
from jax import lax
from jax.experimental import pallas as pl
from jax.experimental.pallas import tpu as pltpu
from jax.sharding import PartitionSpec as P

HD = 128
GROUPS = 8
MAX_HEAD_SPLIT = 4
NEG = -1e30
VMEM = pl.BlockSpec(memory_space=pltpu.VMEM)
ANY = pl.BlockSpec(memory_space=pl.ANY)
SMEM = pl.BlockSpec(memory_space=pltpu.SMEM)


def params(mib):
    return pltpu.CompilerParams(vmem_limit_bytes=mib * 1024 * 1024)


def struct(shape, dtype):
    return jax.ShapeDtypeStruct(shape, dtype)


class Plan:
    def __init__(self, queries):
        self.sections = lax.axis_size("section")
        self.tensors = lax.axis_size("tensor")
        self.rows, self.width = queries.shape
        self.heads = self.width // HD
        self.split = math.gcd(self.heads, MAX_HEAD_SPLIT)
        self.members = self.sections // self.split
        self.cols = self.width // self.split
        self.span = self.sections // GROUPS
        self.share = self.rows // self.tensors
        self.per = 2 if self.span % 2 == 0 and self.members % 2 == 0 else 1
        self.blocks = self.sections // self.per

    def row_starts(self):
        tensor = lax.axis_index("tensor")
        return [(tensor ^ step) * self.share for step in [*range(1, self.tensors), 0]]

    def part(self):
        return lax.axis_index("section") // self.members

    def to_part(self, value, step):
        pairs = [(s, s ^ (step * self.members)) for s in range(self.sections)]
        return lax.ppermute(value, "section", pairs)

    def to_member(self, value, step):
        return lax.ppermute(value, "section", [(s, s ^ step) for s in range(self.sections)])

    def to_tensor(self, value, step):
        return lax.ppermute(value, "tensor", [(t, t ^ step) for t in range(self.tensors)])

    def to_next_group(self, value, step):
        pairs = [
            (s * self.tensors + t, ((s + self.span) % self.sections) * self.tensors + (t ^ step))
            for s in range(self.sections)
            for t in range(self.tensors)
        ]
        return lax.ppermute(value, ("section", "tensor"), pairs)

    def gather_members(self, piece):
        pieces = {0: piece}
        step = self.members // 2
        while step:
            pieces.update({i ^ step: self.to_member(v, step) for i, v in list(pieces.items())})
            step //= 2
        return [pieces[i] for i in range(self.members)]


def pack(plan, step, *arrays):
    at = (plan.part() ^ step) * plan.cols
    return jnp.concatenate([lax.dynamic_slice_in_dim(a, at, plan.cols, 1) for a in arrays], axis=0)


def pack_late_kernel(plan, steps, waits, *refs):
    sources, refs = refs[:3], refs[3 + waits :]
    for step, ref in zip(steps, refs):
        here = pl.ds(pl.multiple_of((plan.part() ^ step) * plan.cols, 128), plan.cols)
        rows = [source[:, here] for source in sources]
        ref[...] = jnp.concatenate(rows, axis=0)[3 * plan.rows - ref.shape[0] :]


def pack_late(plan, steps, arrays, after):
    rows = [(3 if step else 1) * plan.rows for step in steps]
    return pl.pallas_call(
        functools.partial(pack_late_kernel, plan, steps, len(after)),
        out_shape=[struct((n, plan.cols), arrays[0].dtype) for n in rows],
        in_specs=[VMEM] * 3 + [ANY] * len(after),
        out_specs=[VMEM] * len(steps),
        compiler_params=params(4),
    )(*arrays, *after)


def held(values, after):
    def kernel(*refs):
        pass

    return pl.pallas_call(
        kernel,
        out_shape=[struct(v.shape, v.dtype) for v in values],
        in_specs=[ANY] * (len(values) + len(after)),
        out_specs=[ANY] * len(values),
        input_output_aliases={i: i for i in range(len(values))},
        compiler_params=params(1),
    )(*values, *after)


def ready_kernel(plan, waits, order, levels, timesteps, gain, head_weight, *refs):
    shared, bias, delta = refs[waits:]
    count = head_weight.shape[0]
    shared[pl.ds(0, count), :] = head_weight[...]
    rest, rows = gain[...], []
    for _ in range(3):
        rows.append(rest.astype(jnp.bfloat16))
        rest = rest - rows[-1].astype(jnp.float32)
    rows = [jnp.broadcast_to(row, (16, gain.shape[1])) for row in rows]
    shared[pl.ds(count, 48), :] = jnp.concatenate(rows, axis=0)
    me = lax.axis_index("section")
    level = levels[me // plan.span]
    change = (timesteps[level + 1] - timesteps[level]).astype(jnp.float32)
    delta[...] = jnp.full(delta.shape, change, jnp.float32) / 1000.0

    def order_of(step, member):
        return order[(me ^ (step * plan.members + member)) // plan.span]

    for i in range(plan.split):
        for j in range(plan.blocks):
            first = j * plan.per
            seen = order_of(first // plan.members, first % plan.members) <= order_of(i, 0)
            bias[pl.ds(i * plan.blocks + j, 1), :] = jnp.full((1, HD), jnp.where(seen, 0.0, NEG))


def ready(plan, order, levels, timesteps, gain, head_weight, after):
    return pl.pallas_call(
        functools.partial(ready_kernel, plan, len(after)),
        out_shape=[
            struct((head_weight.shape[0] + 48, head_weight.shape[1]), jnp.bfloat16),
            struct((plan.split * plan.blocks, HD), jnp.float32),
            struct((8, HD), jnp.float32),
        ],
        in_specs=[SMEM] * 3 + [VMEM] * 2 + [ANY] * len(after),
        out_specs=[VMEM] * 3,
        compiler_params=params(4),
    )(order, levels, timesteps, gain, head_weight, *after)


def attend_kernel(plan, blocks, begun, last, bias, *refs):
    rows = plan.rows
    before, refs = (refs[:3], refs[3:]) if begun else (None, refs)
    queries, refs = refs[: plan.split], refs[plan.split :]
    pieces, refs = refs[: len(blocks) * plan.per], refs[len(blocks) * plan.per :]
    outs, scores = refs[:-1], refs[-1]
    factor = math.log2(math.e) / math.sqrt(HD)
    width = plan.per * rows

    def hidden(j):
        at = [step * plan.blocks + j for step in range(plan.split)]
        return jnp.concatenate([jnp.broadcast_to(bias[pl.ds(i, 1), :], (rows, HD)) for i in at], axis=0)

    def block(at, which, lanes):
        parts = pieces[at * plan.per : (at + 1) * plan.per]
        return jnp.concatenate([ref[pl.ds(which * rows, rows), lanes] for ref in parts], axis=0)

    for h in range(plan.cols // HD):
        lanes = pl.ds(h * HD, HD)
        q = [
            ref[pl.ds(pl.multiple_of(ref.shape[0] - rows + start, 16), plan.share), lanes]
            for ref in queries
            for start in plan.row_starts()
        ]
        q = jnp.concatenate(q, axis=0)
        top = before[0][h] if begun else None
        for at, j in enumerate(blocks):
            s = lax.dot_general(q, block(at, 0, lanes), (((1,), (1,)), ((), ())), preferred_element_type=jnp.float32)
            scores[:, pl.ds(at * width, width)] = s
            s = functools.reduce(jnp.maximum, [s[:, i : i + HD] for i in range(0, width, HD)])
            s = s + hidden(j)
            top = s if top is None else jnp.maximum(top, s)
        top = jnp.broadcast_to(jnp.max(top, axis=1, keepdims=True), top.shape)
        if begun:
            kept = jnp.exp2((before[0][h] - top) * factor)
            total, summed = kept * before[1][h], kept * before[2][h]
        else:
            total = summed = jnp.zeros(top.shape, jnp.float32)
        for at, j in enumerate(blocks):
            base = top - hidden(j)
            w = [scores[:, pl.ds(at * width + i, HD)] for i in range(0, width, HD)]
            w = [jnp.exp2((s - base) * factor) for s in w]
            total += functools.reduce(jnp.add, w)
            w = jnp.concatenate(w, axis=1).astype(jnp.bfloat16)
            summed += jnp.dot(w, block(at, 1, lanes), preferred_element_type=jnp.float32)
        if last:
            out = (summed / jnp.sum(total, axis=1, keepdims=True)).astype(jnp.bfloat16)
            others = rows - plan.share
            for i, (away, kept) in enumerate(zip(outs[: plan.split], outs[plan.split :])):
                away[:, lanes] = out[i * rows : i * rows + others]
                kept[:, lanes] = out[i * rows + others : (i + 1) * rows]
        else:
            outs[0][h], outs[1][h], outs[2][h] = top, total, summed


def attend(plan, blocks, bias, queries, pieces, state=(), last=False):
    many = plan.split * plan.rows
    shapes = [struct((plan.cols // HD, many, HD), jnp.float32)] * 3
    if last:
        shapes = [struct((plan.rows - plan.share, plan.cols), jnp.bfloat16)] * plan.split
        shapes += [struct((plan.share, plan.cols), jnp.bfloat16)] * plan.split
    pieces = [p for j in blocks for p in pieces[j]]
    out = pl.pallas_call(
        functools.partial(attend_kernel, plan, blocks, bool(state), last),
        out_shape=shapes,
        in_specs=[VMEM] * (1 + len(state) + plan.split + len(pieces)),
        out_specs=[VMEM] * len(shapes),
        scratch_shapes=[pltpu.VMEM((many, len(pieces) * plan.rows), jnp.float32)],
        compiler_params=params(12),
        cost_estimate=pl.CostEstimate(
            flops=16 * many * len(pieces) * plan.rows * plan.cols, bytes_accessed=0, transcendentals=0
        ),
    )(bias, *state, *queries, *pieces)
    return list(out)


def project_kernel(plan, steps, begun, *refs):
    count = len(steps)
    parts, weight, refs = refs[:count], refs[count], refs[count + 1 :]
    outs = refs[1:] if begun else refs
    tile = 512
    for at in range(0, weight.shape[1], tile):
        cols = pl.ds(at, tile)
        total = refs[0][:, cols] if begun else 0.0
        for step, ref in zip(steps, parts):
            here = pl.ds(pl.multiple_of((plan.part() ^ step) * plan.cols, 128), plan.cols)
            total += jnp.dot(ref[...], weight[here, cols], preferred_element_type=jnp.float32)
        rows = total.shape[0] // len(outs)
        for i, out in enumerate(outs):
            out[:, cols] = total[i * rows : (i + 1) * rows].astype(out.dtype)


def project(plan, steps, parts, weight, begun=None, split=False):
    rows, width = parts[0].shape[0], weight.shape[1]
    extra = () if begun is None else (begun,)
    shapes = [struct((rows, width), jnp.float32)]
    if split:
        shapes = [struct((plan.share, width), jnp.bfloat16)] * (rows // plan.share)
    out = pl.pallas_call(
        functools.partial(project_kernel, plan, steps, bool(extra)),
        out_shape=shapes,
        in_specs=[VMEM] * (len(parts) + 1 + len(extra)),
        out_specs=[VMEM] * len(shapes),
        compiler_params=params(8),
        cost_estimate=pl.CostEstimate(flops=0, bytes_accessed=0, transcendentals=0),
    )(*parts, weight, *extra)
    return list(out) if split else out[0]


def head_kernel(plan, delta, *refs):
    sums, refs = refs[: plan.tensors], refs[plan.tensors :]
    shared, refs = refs[: plan.tensors], refs[plan.tensors :]
    latents, velocity_ref, moved_ref, full, rows = refs
    tensor = lax.axis_index("tensor")
    total = sums[0][...]
    for ref in sums[1:]:
        total = total + ref[...].astype(jnp.float32)
    full[...] = total
    squares = jnp.sum(total * total, axis=1, keepdims=True)
    count = rows.shape[1]
    raw = None
    for step, ref in enumerate(shared):
        share = ref.shape[1]
        here = pl.ds(pl.multiple_of((tensor ^ step) * share, 128), share)
        gain = sum(ref[pl.ds(count + 16 * i, 16), :].astype(jnp.float32)[:1] for i in range(3))
        scaled = (full[:, here] * gain).astype(jnp.bfloat16)
        term = lax.dot_general(
            scaled,
            ref[pl.ds(0, count), :],
            (((1,), (1,)), ((), ())),
            preferred_element_type=jnp.float32,
        )
        raw = term if raw is None else raw + term
    rows[...] = raw * lax.rsqrt(squares / total.shape[1] + 1e-6)
    half = plan.share // 2
    velocity = jnp.concatenate(
        [rows[pl.ds(0, half, 2), :], rows[pl.ds(1, half, 2), :]], axis=1
    )
    velocity_ref[...] = velocity
    here = pl.ds(pl.multiple_of(tensor * half, 8), half)
    moved_ref[...] = latents[here, :] + delta[pl.ds(0, 1), :] * velocity


def head(plan, delta, sums, shared, latents):
    half = struct((plan.share // 2, latents.shape[1]), jnp.float32)
    return pl.pallas_call(
        functools.partial(head_kernel, plan),
        out_shape=[half, half],
        in_specs=[VMEM] * (2 * plan.tensors + 2),
        out_specs=[VMEM, VMEM],
        scratch_shapes=[
            pltpu.VMEM(sums[0].shape, jnp.float32),
            pltpu.VMEM((plan.share, latents.shape[1] // 2), jnp.float32),
        ],
        compiler_params=params(12),
    )(delta, *sums, *shared, latents)


def place_kernel(plan, *refs):
    velocities, moved = refs[: plan.tensors], refs[plan.tensors : 2 * plan.tensors]
    tensor = lax.axis_index("tensor")
    for parts, out in ((velocities, refs[-2]), (moved, refs[-1])):
        for step, ref in enumerate(parts):
            rows = ref.shape[0]
            out[pl.ds(pl.multiple_of((tensor ^ step) * rows, 8), rows), :] = ref[...]


def place(plan, velocities, moved):
    shape = struct((plan.rows // 2, velocities[0].shape[1]), jnp.float32)
    return pl.pallas_call(
        functools.partial(place_kernel, plan),
        out_shape=[shape, shape],
        in_specs=[VMEM] * (2 * plan.tensors),
        out_specs=[VMEM, VMEM],
        compiler_params=params(2),
    )(*velocities, *moved)


def local(queries, keys, values, latents, out_weight, gain, head_weight, levels, timesteps, order):
    plan = Plan(queries)
    split, tensors = plan.split, plan.tensors

    far = list(range(1, split))
    own = pack(plan, 0, keys, values)
    if split == 4 and plan.members == 4:
        two = plan.to_part(pack(plan, 2, keys, values, queries), 2)
        one = plan.to_part(pack(plan, 1, keys, values, queries), 1)
        own = plan.gather_members(own)
        late, *asked = pack_late(plan, [3, 0], (keys, values, queries), [own[2]])
        shared, bias, delta = ready(plan, order, levels, timesteps, gain[None, :], head_weight.T, [own[2], late])
        shared = [shared] + [plan.to_tensor(shared, i) for i in range(1, tensors)]
        ones = plan.gather_members(one[: 2 * plan.rows])
        (three,) = held([late], [two, own[2], bias])
        three = plan.to_part(three, 3)
        asked += [one, two, three]
        twos = plan.gather_members(*held([two[: 2 * plan.rows]], []))
        threes = [*held([three[: 2 * plan.rows]], [ones[2], twos[2], *shared[1:]])]
        threes += [plan.to_member(threes[0], i) for i in (1, 2)]
        pairs = [v[i : i + 2] for v in (own, ones, twos) for i in (0, 2)]
        pairs.append(threes[:2])
        state = attend(plan, [0, 2, 4, 6, 1, 3, 5], bias, asked, pairs)
        (last,) = held(threes[2:], [state[0]])
        pairs.append([last, plan.to_member(last, 1)])
        attended = attend(plan, [7], bias, asked, pairs, state, True)
    else:
        shared, bias, delta = ready(plan, order, levels, timesteps, gain[None, :], head_weight.T, [])
        shared = [shared] + [plan.to_tensor(shared, i) for i in range(1, tensors)]
        sent = [own] + [plan.to_part(pack(plan, i, keys, values), i) for i in far]
        asked = [pack(plan, 0, queries)] + [plan.to_part(pack(plan, i, queries), i) for i in far]
        pieces = [p for v in sent for p in plan.gather_members(v)]
        pairs = [pieces[i : i + plan.per] for i in range(0, len(pieces), plan.per)]
        blocks = list(range(plan.blocks))
        own_blocks = blocks[:: plan.blocks // split]
        state = attend(plan, own_blocks, bias, asked, pairs)
        attended = attend(plan, [j for j in blocks if j not in own_blocks], bias, asked, pairs, state, True)

    away, kept = attended[:split], attended[split:]
    away = [plan.to_part(v, i) if i else v for i, v in enumerate(away)]
    near, rest = list(range(split // 2)), list(range(split // 2, split))
    begun = project(plan, near, away[: len(near)], out_weight) if near else None
    away = project(plan, rest, away[len(near) :], out_weight, begun, True)
    away = [plan.to_tensor(v, i + 1) for i, v in enumerate(away)]
    kept = [plan.to_part(v, i) if i else v for i, v in enumerate(kept)]
    begun = project(plan, near, kept[: len(near)], out_weight) if near else None
    sums = [project(plan, rest, kept[len(near) :], out_weight, begun), *away]
    velocity, moved = head(plan, delta, sums, shared, latents)
    advanced = [plan.to_next_group(moved, i) for i in range(tensors)]
    velocities = [velocity] + [plan.to_tensor(velocity, i) for i in range(1, tensors)]
    return place(plan, advanced, velocities)[::-1]


def solution(mesh):
    return jax.shard_map(
        local,
        mesh=mesh,
        in_specs=(
            P("section", "tensor"),
            P("section", "tensor"),
            P("section", "tensor"),
            P("section", None),
            P("tensor", None),
            P("tensor"),
            P("tensor", None),
            P(),
            P(),
            P(),
        ),
        out_specs=(P("section", None), P("section", None)),
        check_vma=False,
    )
```
